32 devices in a mesh: groups: 2 (over x), dev: 16 (over z, y, core).
Axes of the slice: x: 2, y: 2, z: 4, core: 2. Of those that a mesh axis runs over, the one named last changes fastest.
Arguments:
- queries: bfloat16 [1024, 4096], P(('groups', 'dev')), parts along dimension 0, may hold values from -6 to 6
- keys: bfloat16 [1024, 160, 256], P(('groups', 'dev')), parts along dimension 0, may hold values from -6 to 6
- values: bfloat16 [1024, 160, 256], P(('groups', 'dev')), parts along dimension 0, may hold values from -6 to 6
- lengths: int32 [1024], P(('groups', 'dev')), parts along dimension 0, may hold values from 2 to 160, as said below
- residual: bfloat16 [1024, 4096], P(('groups', 'dev')), parts along dimension 0, may hold values from -36 to 36
- out_weight: bfloat16 [4096, 4096], P(None, 'dev'), may hold values from -0.09375 to 0.09375
- norm_gain: bfloat16 [4096], replicated, may hold values from 0.099609375 to 1.8984375
- expert_ids: int32 [1024, 8], P(('groups', 'dev')), parts along dimension 0, may hold values from 0 to 15, all different within a row; in each aligned block of 32 rows (0 to 31, 32 to 63, ...) at most 32 rows name the same one
- routed_gate_weight: float32 [1024, 8], P(('groups', 'dev')), parts along dimension 0, may hold values from 0.05 to 0.5
- w_gate: bfloat16 [16, 4096, 768], P('dev'), may hold values from -0.09375 to 0.09375
- w_up: bfloat16 [16, 4096, 768], P('dev'), may hold values from -0.09375 to 0.09375
- w_down: bfloat16 [16, 768, 4096], P('dev'), may hold values from -0.21875 to 0.21875
Outputs:
- layer_out: bfloat16 [1024, 4096], P(('groups', 'dev')), parts along dimension 0
The draws below stay inside these ranges and needn't reach their ends.
There are 2 independent parts, one for each index of `groups`. The reference program is written for one: setup_inputs(seed, part) draws one part's arguments, and reference() takes and returns one part's arrays. A program takes and returns all parts, laid end to end along the dimension named above; an argument that names none is the same for every part. Nothing has to cross between parts.
Inputs may be any that keep to these rules, and one draw needn't show every extreme that they name: `lengths`: some sequence has 160 live positions. `expert_ids`: each token names 8 different experts; among the 32 tokens of one index of dev (aligned blocks of rows) no expert is named more than 32 times, a bound that some block reaches.
All inputs are finite; a program needn't handle non-finite values.
Results may differ from the reference program's by a relative error of at most 0.006.
Values may be sent and summed in bfloat16 or wider, within the bound.
A program may use at most 128 MiB of HBM per device.

```python
import math
import jax
import jax.numpy as jnp
import numpy as np
from jax import lax

D = 4096
HQ = 32
KVH = 2
HD = 128
FF = 768
TOPK = 8
T_DEV = 32
LMAX = 160
BATCH = 512
EXPERTS = 16
CAP = 32
N_DEV = 16


def draw_queries(key, part):
    key = jax.random.fold_in(key, 11)
    base = jnp.clip(jax.random.normal(key, (BATCH, HQ, HD), jnp.float32), -6.0, 6.0)
    return base.reshape(BATCH, HQ * HD).astype(jnp.bfloat16)


def draw_keys(key, part):
    key = jax.random.fold_in(key, 12)
    base = jnp.clip(jax.random.normal(key, (BATCH, LMAX, KVH, HD), jnp.float32), -6.0, 6.0)
    return base.reshape(BATCH, LMAX, KVH * HD).astype(jnp.bfloat16)


def draw_lengths(key, part):
    key = jax.random.fold_in(key, 5)
    key_one, key_two = jax.random.split(key)
    spans = jax.random.randint(key_one, (BATCH,), 2, LMAX + 1)
    spot = jax.random.randint(key_two, (), 0, BATCH)
    return jnp.where(jnp.arange(BATCH) == spot, LMAX, spans).astype(jnp.int32)


def draw_residual(key, part):
    key = jax.random.fold_in(key, 13)
    keys_three = jax.random.split(key, 3)
    row_norm_factor = jnp.exp(jax.random.uniform(keys_three[0], (BATCH, 1), jnp.float32, math.log(0.3), math.log(3.0)))
    col_scale = jnp.exp(jax.random.uniform(keys_three[1], (1, D), jnp.float32, math.log(0.3), math.log(3.0)))
    base = jnp.clip(jax.random.normal(keys_three[2], (BATCH, D), jnp.float32), -4.0, 4.0)
    return (base * row_norm_factor * col_scale).astype(jnp.bfloat16)


def levels(key, shape, cuts, smallest, largest):
    def one(axis_at, blocks):
        draws = jax.random.uniform(jax.random.fold_in(jax.random.fold_in(key, 6), axis_at), (blocks,), jnp.float32, smallest / len(cuts), largest / len(cuts))
        return jnp.repeat(jnp.exp(draws), shape[axis_at] // blocks).reshape((-1,) + (1,) * (len(shape) - axis_at - 1))

    loudness = one(*cuts[0])
    for cut in cuts[1:]:
        loudness = loudness * one(*cut)
    return loudness


def routed_block(rng, own, number, rows, count, top, most, skew):
    sequence = jax.random.permutation(rng, count)
    heavy_load, common = load_shares(count, rows * top, most, skew, True), load_shares(count, rows * top, most, skew, False)
    places = jnp.arange(count)

    def named(sizes, turn):
        used = int((sizes > 0).sum())
        fixed = max(1, used // 4)
        shifted = fixed + (places - fixed + turn * (used - fixed)) % max(1, count - fixed)
        return jnp.zeros((count,), jnp.int32).at[sequence[jnp.where(places < fixed, places, shifted)]].set(jnp.asarray(sizes, jnp.int32))

    sizes = jnp.where(number % 4 == 0, named(heavy_load, number // 4), named(common, number - number // 4 - 1))
    mixed = jax.random.permutation(jax.random.fold_in(own, 3), count)
    giver, taker = mixed[0:count // 2 * 2:2], mixed[1:count // 2 * 2:2]
    margin = jnp.minimum(sizes[giver] - 1, most - sizes[taker]) // 2
    margin = jnp.where((giver == sequence[0]) | (taker == sequence[0]) | (sizes[taker] == 0), 0, jnp.maximum(margin, 0))
    shifted = jax.random.randint(jax.random.fold_in(own, 4), (count // 2,), 0, 1 << 20) % (margin + 1)
    sizes = sizes.at[giver].add(-shifted).at[taker].add(shifted)
    members = jnp.searchsorted(jnp.cumsum(sizes), jnp.arange(rows * top), side="right").astype(jnp.int32)
    table = members.reshape(top, rows).T
    table = table[jax.random.permutation(jax.random.fold_in(own, 1), rows)]
    turn = jax.random.randint(jax.random.fold_in(own, 2), (rows, 1), 0, top)
    return jnp.take_along_axis(table, (jnp.arange(top)[None, :] + turn) % top, axis=1)


def load_shares(number_of, total, reach, slope, full):
    loads = [(1 << 20) // math.isqrt(grade ** slope) + 1 for grade in range(1, number_of + 1)]
    largest = reach if full else min(reach, max(-(-total // number_of), total * loads[0] // sum(loads)))
    least = 1 if total - largest >= number_of - 1 else 0
    holding, spare = [largest] + [least] * (number_of - 1), total - largest - least * (number_of - 1)
    while spare > 0:
        candidates = [i for i in range(1, number_of) if holding[i] < largest] or [i for i in range(1, number_of) if holding[i] < reach]
        whole, remaining = sum([loads[i] for i in candidates]), spare
        for i in candidates:
            extra = min(reach - holding[i], max(1, remaining * loads[i] // whole), spare)
            holding[i] = holding[i] + extra
            spare = spare - extra
    return np.array(holding)


def scatter_about(rng, shape, deviation, bound, pieces=(), held_as=jnp.bfloat16):
    array = deviation * jax.random.normal(rng, shape, jnp.float32)
    if pieces:
        array = array * levels(rng, shape, pieces, -0.22, 0.18)
    return jnp.clip(array, -bound, bound).astype(held_as)


def setup_inputs(seed: int = 0, part: int = 0) -> dict:
    arg_keys = jax.random.split(jax.random.key(seed), 13)
    own_keys = jax.random.split(jax.random.fold_in(arg_keys[12], part), 13)
    queries = draw_queries(jax.random.fold_in(jax.random.fold_in(arg_keys[12], part), 71), part)
    keys = draw_keys(jax.random.fold_in(jax.random.fold_in(arg_keys[12], part), 71), part)
    values = scatter_about(own_keys[2], (BATCH, LMAX, KVH * HD), 1.0, 6.0, ((0, 16),))
    lengths = draw_lengths(jax.random.fold_in(jax.random.fold_in(arg_keys[12], part), 71), part)
    residual = draw_residual(jax.random.fold_in(jax.random.fold_in(arg_keys[12], part), 71), part)
    out_weight = scatter_about(arg_keys[5], (HQ * HD, D), (HQ * HD) ** -0.5, 0.09375, ((1, 16),))
    norm_gain = jnp.clip(1.0 + 0.18 * jax.random.normal(arg_keys[6], (D,), jnp.float32), 0.099609375, 1.8984375).astype(jnp.bfloat16)
    expert_ids_keys = jax.random.split(jax.random.fold_in(own_keys[7], 1), BATCH // T_DEV)
    expert_ids_turns = jax.random.permutation(jax.random.fold_in(own_keys[7], 3), BATCH // T_DEV)
    expert_ids = jax.vmap(lambda own, number: routed_block(jax.random.fold_in(own_keys[7], 2), own, number, T_DEV, EXPERTS, TOPK, CAP, 2))(expert_ids_keys, expert_ids_turns).reshape((BATCH, TOPK))
    routed_gate_weight = jnp.clip(jnp.exp(math.log(0.5) - 2.3025851 * jax.random.uniform(own_keys[8], (BATCH, TOPK), jnp.float32) ** levels(own_keys[8], (BATCH, TOPK), ((0, 16),), -0.2, 0.2)), 0.05, 0.5)
    w_gate = scatter_about(arg_keys[9], (EXPERTS, D, FF), D ** -0.5, 0.09375, ((0, 16),))
    w_up = scatter_about(arg_keys[10], (EXPERTS, D, FF), D ** -0.5, 0.09375, ((0, 16),))
    w_down = scatter_about(arg_keys[11], (EXPERTS, FF, D), FF ** -0.5, 0.21875, ((0, 16),))
    return dict(queries=queries, keys=keys, values=values, lengths=lengths, residual=residual, out_weight=out_weight, norm_gain=norm_gain, expert_ids=expert_ids, routed_gate_weight=routed_gate_weight, w_gate=w_gate, w_up=w_up, w_down=w_down)


def attend(queries, keys, values, lengths):
    seq_rows = queries.shape[0]
    token_position_index = keys.shape[1]
    query_heads = queries.reshape(seq_rows, KVH, HQ // KVH, HD).astype(jnp.float32)
    key_heads = keys.reshape(seq_rows, token_position_index, KVH, HD).astype(jnp.float32)
    value_heads = values.reshape(seq_rows, token_position_index, KVH, HD).astype(jnp.float32)
    scores = jnp.einsum('bgqd,bpgd->bgqp', query_heads, key_heads, precision=lax.Precision.HIGHEST) * (1.0 / math.sqrt(HD))
    live = jnp.arange(token_position_index, dtype=jnp.int32)[None, None, None, :] < lengths[:, None, None, None]
    scores = jnp.where(live, scores, jnp.float32(-1e+30))
    highest = lax.optimization_barrier(jnp.max(scores, axis=-1, keepdims=True))
    weights = jnp.exp(scores - highest)
    probs = (weights / lax.optimization_barrier(jnp.sum(weights, axis=-1, keepdims=True))).astype(jnp.bfloat16)
    mixed = jnp.einsum('bgqp,bpgd->bgqd', probs.astype(jnp.float32), value_heads, precision=lax.Precision.HIGHEST)
    return mixed.reshape(seq_rows, HQ * HD).astype(jnp.bfloat16)

def reference(queries, keys, values, lengths, residual, out_weight, norm_gain, expert_ids, routed_gate_weight, w_gate, w_up, w_down):
    attended = attend(queries, keys, values, lengths)
    projected = jnp.dot(attended, out_weight, preferred_element_type=jnp.float32).astype(jnp.bfloat16)
    stream = residual.astype(jnp.float32) + projected.astype(jnp.float32)
    scale = lax.rsqrt(lax.optimization_barrier(jnp.mean(stream * stream, axis=-1, keepdims=True)) + 1e-06)
    normalized_input = (stream * scale * norm_gain.astype(jnp.float32)).astype(jnp.bfloat16)
    flattened_expert_index = expert_ids.reshape(-1)
    total_pairs = flattened_expert_index.shape[0]
    room = N_DEV * CAP

    def one_expert(index):
        hits = flattened_expert_index == index
        chosen = jnp.nonzero(hits, size=room, fill_value=0)[0].astype(jnp.int32)
        live = jnp.arange(room, dtype=jnp.int32) < jnp.sum(hits.astype(jnp.int32))
        row_block = normalized_input[chosen // TOPK]
        gate_part = jnp.dot(row_block, w_gate[index], preferred_element_type=jnp.float32)
        up_part = jnp.dot(row_block, w_up[index], preferred_element_type=jnp.float32)
        inner = (jax.nn.silu(gate_part) * up_part).astype(jnp.bfloat16)
        result = jnp.dot(inner, w_down[index], preferred_element_type=jnp.float32).astype(jnp.bfloat16)
        target = jnp.where(live, chosen, jnp.int32(total_pairs))
        return (target, result)
    targets, results = lax.map(one_expert, jnp.arange(EXPERTS, dtype=jnp.int32))
    slots = jnp.zeros((total_pairs + 1, D), jnp.bfloat16).at[targets.reshape(-1)].set(results.reshape(-1, D))
    selected_experts = slots[:total_pairs].reshape(BATCH, TOPK, D).astype(jnp.float32)
    mixed_expert_output = jnp.einsum('cz,czw->cw', routed_gate_weight.astype(jnp.float32), selected_experts, precision=lax.Precision.HIGHEST)
    return (stream + mixed_expert_output).astype(jnp.bfloat16)
```

```python
import math

import jax
import jax.numpy as jnp
from jax import lax
from jax.sharding import PartitionSpec as P

HQ = 32
KVH = 2
HD = 128


def attend(queries, keys, values, lengths):
    seq_rows = queries.shape[0]
    token_position_index = keys.shape[1]
    query_heads = queries.reshape(seq_rows, KVH, HQ // KVH, HD)
    key_heads = keys.reshape(seq_rows, token_position_index, KVH, HD)
    value_heads = values.reshape(seq_rows, token_position_index, KVH, HD)
    scores = jnp.einsum(
        "bgqd,bpgd->bgqp", query_heads, key_heads, preferred_element_type=jnp.float32
    ) * (1.0 / math.sqrt(HD))
    live = (
        jnp.arange(token_position_index, dtype=jnp.int32)[None, None, None, :]
        < lengths[:, None, None, None]
    )
    scores = jnp.where(live, scores, jnp.float32(-1e30))
    highest = jnp.max(scores, axis=-1, keepdims=True)
    weights = jnp.exp(scores - highest)
    probs = (weights / jnp.sum(weights, axis=-1, keepdims=True)).astype(jnp.bfloat16)
    mixed = jnp.einsum("bgqp,bpgd->bgqd", probs, value_heads, preferred_element_type=jnp.float32)
    return mixed.reshape(seq_rows, HQ * HD).astype(jnp.bfloat16)


def expert_rows(row_block, w_gate, w_up, w_down):
    gate_part = jnp.dot(row_block, w_gate[0], preferred_element_type=jnp.float32)
    up_part = jnp.dot(row_block, w_up[0], preferred_element_type=jnp.float32)
    inner = (jax.nn.silu(gate_part) * up_part).astype(jnp.bfloat16)
    return jnp.dot(inner, w_down[0], preferred_element_type=jnp.float32).astype(jnp.bfloat16)


def per_device(
    queries,
    keys,
    values,
    lengths,
    residual,
    out_weight,
    norm_gain,
    expert_ids,
    routed_gate_weight,
    w_gate,
    w_up,
    w_down,
):
    attended = attend(queries, keys, values, lengths)
    attended_all = lax.all_gather(attended, "dev", axis=0, tiled=True)
    columns = jnp.dot(attended_all, out_weight, preferred_element_type=jnp.float32).astype(
        jnp.bfloat16
    )
    projected = lax.all_to_all(columns, "dev", split_axis=0, concat_axis=1, tiled=True)
    stream = residual.astype(jnp.float32) + projected.astype(jnp.float32)
    scale = lax.rsqrt(jnp.mean(stream * stream, axis=-1, keepdims=True) + 1e-06)
    normed = (stream * scale * norm_gain.astype(jnp.float32)).astype(jnp.bfloat16)
    expert_count = lax.axis_size("dev")
    experts = jnp.arange(expert_count, dtype=jnp.int32)
    named = expert_ids[:, :, None] == experts[None, None, :]
    share = jnp.sum(jnp.where(named, routed_gate_weight[:, :, None], 0.0), axis=1)
    mine = lax.all_to_all(share.T, "dev", split_axis=0, concat_axis=0, tiled=True).reshape(-1)
    normed_all = lax.all_gather(normed, "dev", axis=0, tiled=True)
    rows = expert_rows(normed_all, w_gate, w_up, w_down)
    weighted = (rows.astype(jnp.float32) * mine[:, None]).astype(jnp.bfloat16)
    mixed = lax.psum_scatter(weighted, "dev", scatter_dimension=0, tiled=True)
    return (stream + mixed.astype(jnp.float32)).astype(jnp.bfloat16)


def solution(mesh):
    in_specs = (
        P(("groups", "dev"), None),
        P(("groups", "dev"), None, None),
        P(("groups", "dev"), None, None),
        P(("groups", "dev")),
        P(("groups", "dev"), None),
        P(None, "dev"),
        P(),
        P(("groups", "dev"), None),
        P(("groups", "dev"), None),
        P("dev", None, None),
        P("dev", None, None),
        P("dev", None, None),
    )
    out_specs = P(("groups", "dev"), None)
    return jax.shard_map(
        per_device, mesh=mesh, in_specs=in_specs, out_specs=out_specs, check_vma=False
    )
```

```python
import functools
import math

import jax
import jax.numpy as jnp
from jax import lax
from jax.experimental import pallas as pl
from jax.experimental.pallas import tpu as pltpu
from jax.sharding import PartitionSpec as P

HQ = 32
KVH = 2
HD = 128


def attend(queries, keys, values, lengths):
    seq_rows = queries.shape[0]
    token_position_index = keys.shape[1]
    query_heads = queries.reshape(seq_rows, KVH, HQ // KVH, HD)
    key_heads = keys.reshape(seq_rows, token_position_index, KVH, HD)
    value_heads = values.reshape(seq_rows, token_position_index, KVH, HD)
    scores = jnp.einsum(
        "bgqd,bpgd->bgqp", query_heads, key_heads, preferred_element_type=jnp.float32
    ) * (1.0 / math.sqrt(HD))
    live = (
        jnp.arange(token_position_index, dtype=jnp.int32)[None, None, None, :]
        < lengths[:, None, None, None]
    )
    scores = jnp.where(live, scores, jnp.float32(-1e30))
    highest = jnp.max(scores, axis=-1, keepdims=True)
    weights = jnp.exp(scores - highest)
    probs = (weights / jnp.sum(weights, axis=-1, keepdims=True)).astype(jnp.bfloat16)
    mixed = jnp.einsum("bgqp,bpgd->bgqd", probs, value_heads, preferred_element_type=jnp.float32)
    return mixed.reshape(seq_rows, HQ * HD).astype(jnp.bfloat16)


MESH = pl.DeviceIdType.MESH
HALVES = 2
UP, DOWN, ACROSS, SIBLING = 0, 1, 2, 3


def layer_kernel(
    n,
    attended,
    residual,
    gain,
    share,
    out_weight,
    w_gate,
    w_up,
    w_down,
    out,
    rows_one,
    rows_two,
    cols,
    arrived,
    share_in,
    stream,
    inner,
    part,
    from_sib,
    from_y,
    from_below,
    from_above,
    v_out,
    v_gate,
    v_up,
    v_down,
    load_sem,
    send_one,
    recv_one,
    send_two,
    recv_two,
    col_send,
    col_recv,
    share_send,
    share_recv,
    sib_send,
    sib_recv,
    y_send,
    y_recv,
    up_send,
    up_recv,
    down_send,
    down_recv,
):
    me = lax.axis_index("dev")
    depth = n // 4
    z, y, k = me // 4, (me // 2) % 2, me % 2
    t_dev = attended.shape[0]
    half = t_dev // HALVES
    width = out_weight.shape[1]
    ff = w_gate.shape[1]
    model = attended.shape[1]

    def at(zz, yy, kk):
        return zz * 4 + yy * 2 + kk

    sib, beside = at(z, y, 1 - k), at(z, 1 - y, k)

    def remote(src, dst, send, recv, target):
        return pltpu.make_async_remote_copy(
            src_ref=src,
            dst_ref=dst,
            send_sem=send,
            recv_sem=recv,
            device_id={"dev": target},
            device_id_type=MESH,
        )

    loads = [
        pltpu.make_async_copy(out_weight, v_out, load_sem.at[0]),
        pltpu.make_async_copy(w_gate, v_gate, load_sem.at[1]),
        pltpu.make_async_copy(w_up, v_up, load_sem.at[2]),
        pltpu.make_async_copy(w_down, v_down, load_sem.at[3]),
    ]
    for load in loads:
        load.start()
    rows_one[me] = attended[...]

    barrier = pltpu.get_barrier_semaphore()

    def greet(i, _):
        pl.semaphore_signal(
            barrier, inc=1, device_id={"dev": lax.rem(me + i, n)}, device_id_type=MESH
        )
        return 0

    lax.fori_loop(1, n, greet, 0)
    pl.semaphore_wait(barrier, n - 1)

    def order(j):
        near = jnp.minimum(z, depth - 1 - z)
        both = j <= 2 * near
        dist = jnp.where(both, (j + 1) // 2, j - near)
        rising = jnp.where(z < depth - 1 - z, 1, -1)
        sign = jnp.where(both, jnp.where(j % 2 == 1, -1, 1), rising)
        return z + sign * dist

    def gather(buf, send, recv, use):
        def copy(b, h, way, target):
            piece = buf.at[b, pl.ds(h * half, half), :]
            return remote(piece, piece, send.at[b, h, way], recv.at[b, h], target)

        def sends(zj, b, h, act):
            @pl.when((zj <= z) & (z < depth - 1))
            def _():
                act(copy(b, h, UP, at(z + 1, y, k)))

            @pl.when((zj >= z) & (z > 0))
            def _():
                act(copy(b, h, DOWN, at(z - 1, y, k)))

            act(copy(b, h, ACROSS, beside))
            act(copy(b, h, SIBLING, sib))

        def stage(j, _):
            @pl.when(j < depth)
            def _():
                zj = order(j)
                b = at(zj, y, k)
                for h in range(HALVES):

                    @pl.when(j > 0)
                    def _():
                        copy(b, h, SIBLING, sib).wait_recv()

                    sends(zj, b, h, lambda c: c.start())

            @pl.when((j >= 1) & (j <= depth))
            def _():
                b = at(order(j - 1), 1 - y, k)
                for h in range(HALVES):
                    copy(b, h, SIBLING, sib).wait_recv()
                    copy(b, h, SIBLING, sib).start()

            @pl.when(j >= 2)
            def _():
                zj = order(j - 2)
                for yy in range(2):
                    for h in range(HALVES):
                        copy(at(zj, yy, 1 - k), h, SIBLING, sib).wait_recv()
                use(zj)

            return 0

        lax.fori_loop(0, depth + 2, stage, 0)

        def drain():
            def one(j, _):
                zj = order(j)
                for h in range(HALVES):
                    sends(zj, at(zj, y, k), h, lambda c: c.wait_send())
                    copy(at(zj, 1 - y, k), h, SIBLING, sib).wait_send()
                return 0

            lax.fori_loop(0, depth, one, 0)

        return drain

    def share_copy(b, slot):
        return remote(share.at[b], share_in.at[slot], share_send.at[b], share_recv.at[slot], b)

    def col_copy(b, slot):
        return remote(cols.at[b], arrived.at[slot], col_send.at[b], col_recv.at[slot], b)

    share_in[me] = share[me]

    def give_share(i, _):
        share_copy(lax.rem(me + i, n), me).start()
        return 0

    lax.fori_loop(1, n, give_share, 0)
    loads[0].wait()

    def project(zj):
        x = rows_one[pl.ds(zj * 4, 4)].reshape(4 * t_dev, model)
        c = jnp.dot(x, v_out[...], preferred_element_type=jnp.float32).astype(jnp.bfloat16)
        cols[pl.ds(zj * 4, 4)] = c.reshape(4, t_dev, width)
        for q in range(4):
            b = zj * 4 + q

            @pl.when(b != me)
            def _():
                col_copy(b, me).start()

    drain_one = gather(rows_one, send_one, recv_one, project)
    arrived[me] = cols[me]

    def take(i, _):
        s = lax.rem(me + i, n)
        col_copy(s, s).wait_recv()
        share_copy(s, s).wait_recv()
        return 0

    lax.fori_loop(1, n, take, 0)
    squares = jnp.zeros((t_dev, width), jnp.float32)
    for s in range(n):
        cut = pl.ds(s * width, width)
        piece = residual[:, cut].astype(jnp.float32) + arrived[s].astype(jnp.float32)
        stream[:, cut] = piece
        squares += piece * piece
    scale = lax.rsqrt(jnp.sum(squares, axis=1, keepdims=True) * (1.0 / model) + 1e-06)
    for s in range(n):
        cut = pl.ds(s * width, width)
        rows_two[me, :, cut] = (
            stream[:, cut] * scale * gain[:, cut].astype(jnp.float32)
        ).astype(jnp.bfloat16)
    for load in loads[1:]:
        load.wait()

    def sib_copy(b):
        return remote(part.at[b], from_sib.at[b], sib_send.at[b], sib_recv.at[b], sib)

    tile, wide = 256, 512
    lanes = share_in.shape[2]
    eye = lax.broadcasted_iota(jnp.int32, (t_dev, lanes), 0) == lax.broadcasted_iota(
        jnp.int32, (t_dev, lanes), 1
    )

    def expert(zj):
        def hidden(t, _):
            x = rows_two[pl.ds(zj * 4, 4)].reshape(4 * t_dev, model)
            cut = pl.ds(pl.multiple_of(t * tile, tile), tile)
            g = jnp.dot(x, v_gate[:, cut], preferred_element_type=jnp.float32)
            u = jnp.dot(x, v_up[:, cut], preferred_element_type=jnp.float32)
            inner[:, cut] = (g / (1.0 + jnp.exp(-g)) * u).astype(jnp.bfloat16)
            return 0

        lax.fori_loop(0, ff // tile, hidden, 0)
        weights = jnp.concatenate(
            [
                jnp.sum(
                    jnp.where(eye, share_in[zj * 4 + q, 0:1, :], 0.0), axis=1, keepdims=True
                )
                for q in range(4)
            ],
            axis=0,
        )

        def outward(t, _):
            cut = pl.ds(pl.multiple_of(t * wide, wide), wide)
            o = jnp.dot(inner[...], v_down[:, cut], preferred_element_type=jnp.float32)
            part[pl.ds(zj * 4, 4), :, cut] = (
                (o * weights).astype(jnp.bfloat16).reshape(4, t_dev, wide)
            )
            return 0

        lax.fori_loop(0, model // wide, outward, 0)
        for yy in range(2):
            sib_copy(at(zj, yy, 1 - k)).start()

    drain_two = gather(rows_two, send_two, recv_two, expert)

    def add(b, other):
        part[b] = (part[b].astype(jnp.float32) + other.astype(jnp.float32)).astype(jnp.bfloat16)

    def y_copy(zb):
        return remote(part.at[at(zb, 1 - y, k)], from_y.at[zb], y_send.at[zb], y_recv.at[zb], beside)

    def up_copy(zb):
        return remote(
            part.at[at(zb, y, k)], from_below.at[zb], up_send.at[zb], up_recv.at[zb], at(z + 1, y, k)
        )

    def down_copy(zb):
        return remote(
            part.at[at(zb, y, k)], from_above.at[zb], down_send.at[zb], down_recv.at[zb], at(z - 1, y, k)
        )

    def sides(t, act):
        @pl.when(z + t < depth)
        def _():
            act(z + t, True)

        @pl.when(z - t >= 0)
        def _():
            act(z - t, False)

    def cross(zb):
        for yy in (0, 1):
            sib_copy(at(zb, yy, k)).wait_recv()
        away = at(zb, 1 - y, k)
        add(away, from_sib[away])
        y_copy(zb).start()
        here = at(zb, y, k)
        add(here, from_sib[here])

    def cross_level(i, _):
        sides(depth - 1 - i, lambda zb, rising: cross(zb))
        return 0

    lax.fori_loop(0, depth - 1, cross_level, 0)
    cross(z)

    def along(zb, rising):
        y_copy(zb).wait_recv()
        here = at(zb, y, k)
        add(here, from_y[zb])
        if rising:

            @pl.when(z > 0)
            def _():
                up_copy(zb).wait_recv()
                add(here, from_below[zb])

            up_copy(zb).start()
        else:

            @pl.when(z < depth - 1)
            def _():
                down_copy(zb).wait_recv()
                add(here, from_above[zb])

            down_copy(zb).start()

    def along_level(i, _):
        sides(depth - 1 - i, along)
        return 0

    lax.fori_loop(0, depth - 1, along_level, 0)
    y_copy(z).wait_recv()
    stream[...] += part[me].astype(jnp.float32) + from_y[z].astype(jnp.float32)

    @pl.when(z > 0)
    def _():
        up_copy(z).wait_recv()
        stream[...] += from_below[z].astype(jnp.float32)

    @pl.when(z < depth - 1)
    def _():
        down_copy(z).wait_recv()
        stream[...] += from_above[z].astype(jnp.float32)

    out[...] = stream[...].astype(jnp.bfloat16)

    drain_one()
    drain_two()

    def sent(i, _):
        b = lax.rem(me + i, n)
        share_copy(b, me).wait_send()
        col_copy(b, me).wait_send()
        return 0

    lax.fori_loop(1, n, sent, 0)

    def sent_line(zb, _):
        for yy in range(2):
            sib_copy(at(zb, yy, 1 - k)).wait_send()
        y_copy(zb).wait_send()

        @pl.when(zb > z)
        def _():
            up_copy(zb).wait_send()

        @pl.when(zb < z)
        def _():
            down_copy(zb).wait_send()

        return 0

    lax.fori_loop(0, depth, sent_line, 0)


def per_device(
    queries,
    keys,
    values,
    lengths,
    residual,
    out_weight,
    norm_gain,
    expert_ids,
    routed_gate_weight,
    w_gate,
    w_up,
    w_down,
):
    n = lax.axis_size("dev")
    depth = n // 4
    t_dev, model = residual.shape
    width = out_weight.shape[1]
    ff = w_gate.shape[2]
    attended = attend(queries, keys, values, lengths)
    experts = jnp.arange(n, dtype=jnp.int32)
    named = expert_ids[None, :, :] == experts[:, None, None]
    share = jnp.sum(jnp.where(named, routed_gate_weight[None], 0.0), axis=2)
    share = jnp.zeros((n, 8, 128), jnp.float32).at[:, 0, :t_dev].set(share)
    vmem, anywhere = pl.BlockSpec(memory_space=pltpu.VMEM), pl.BlockSpec(memory_space=pl.ANY)
    b16, f32 = jnp.bfloat16, jnp.float32
    dma = pltpu.SemaphoreType.DMA
    return pl.pallas_call(
        functools.partial(layer_kernel, n),
        out_shape=jax.ShapeDtypeStruct((t_dev, model), b16),
        in_specs=[vmem] * 4 + [anywhere] * 4,
        out_specs=vmem,
        scratch_shapes=[
            pltpu.VMEM((n, t_dev, model), b16),
            pltpu.VMEM((n, t_dev, model), b16),
            pltpu.VMEM((n, t_dev, width), b16),
            pltpu.VMEM((n, t_dev, width), b16),
            pltpu.VMEM((n, 8, 128), f32),
            pltpu.VMEM((t_dev, model), f32),
            pltpu.VMEM((4 * t_dev, ff), b16),
            pltpu.VMEM((n, t_dev, model), b16),
            pltpu.VMEM((n, t_dev, model), b16),
            pltpu.VMEM((depth, t_dev, model), b16),
            pltpu.VMEM((depth, t_dev, model), b16),
            pltpu.VMEM((depth, t_dev, model), b16),
            pltpu.VMEM((model, width), b16),
            pltpu.VMEM((model, ff), b16),
            pltpu.VMEM((model, ff), b16),
            pltpu.VMEM((ff, model), b16),
            dma((4,)),
            dma((n, HALVES, 4)),
            dma((n, HALVES)),
            dma((n, HALVES, 4)),
            dma((n, HALVES)),
            dma((n,)),
            dma((n,)),
            dma((n,)),
            dma((n,)),
            dma((n,)),
            dma((n,)),
            dma((depth,)),
            dma((depth,)),
            dma((depth,)),
            dma((depth,)),
            dma((depth,)),
            dma((depth,)),
        ],
        compiler_params=pltpu.CompilerParams(
            collective_id=0, has_side_effects=True, vmem_limit_bytes=62 * 1024 * 1024
        ),
    )(
        attended,
        residual,
        norm_gain.reshape(1, model),
        share,
        out_weight,
        w_gate[0],
        w_up[0],
        w_down[0],
    )


def solution(mesh):
    in_specs = (
        P(("groups", "dev"), None),
        P(("groups", "dev"), None, None),
        P(("groups", "dev"), None, None),
        P(("groups", "dev")),
        P(("groups", "dev"), None),
        P(None, "dev"),
        P(),
        P(("groups", "dev"), None),
        P(("groups", "dev"), None),
        P("dev", None, None),
        P("dev", None, None),
        P("dev", None, None),
    )
    out_specs = P(("groups", "dev"), None)
    return jax.shard_map(
        per_device, mesh=mesh, in_specs=in_specs, out_specs=out_specs, check_vma=False
    )
```

```python
import functools
import math

import jax
import jax.numpy as jnp
from jax import lax
from jax.experimental import pallas as pl
from jax.experimental.pallas import tpu as pltpu
from jax.sharding import PartitionSpec as P

HQ = 32
KVH = 2
HD = 128


def attend(queries, keys, values, lengths):
    seq_rows = queries.shape[0]
    token_position_index = keys.shape[1]
    query_heads = queries.reshape(seq_rows, KVH, HQ // KVH, HD)
    key_heads = keys.reshape(seq_rows, token_position_index, KVH, HD)
    value_heads = values.reshape(seq_rows, token_position_index, KVH, HD)
    scores = jnp.einsum(
        "bgqd,bpgd->bgqp", query_heads, key_heads, preferred_element_type=jnp.float32
    ) * (1.0 / math.sqrt(HD))
    live = (
        jnp.arange(token_position_index, dtype=jnp.int32)[None, None, None, :]
        < lengths[:, None, None, None]
    )
    scores = jnp.where(live, scores, jnp.float32(-1e30))
    highest = jnp.max(scores, axis=-1, keepdims=True)
    weights = jnp.exp(scores - highest)
    probs = (weights / jnp.sum(weights, axis=-1, keepdims=True)).astype(jnp.bfloat16)
    mixed = jnp.einsum("bgqp,bpgd->bgqd", probs, value_heads, preferred_element_type=jnp.float32)
    return mixed.reshape(seq_rows, HQ * HD).astype(jnp.bfloat16)


MESH = pl.DeviceIdType.MESH
HALVES = 2
UP, DOWN, ACROSS, SIBLING = 0, 1, 2, 3


def layer_kernel(
    n,
    attended,
    residual,
    gain,
    share,
    out_weight,
    w_gate,
    w_up,
    w_down,
    out,
    rows_one,
    rows_two,
    cols,
    arrived,
    share_in,
    stream,
    inner,
    part,
    from_sib,
    from_y,
    from_below,
    from_above,
    v_out,
    v_gate,
    v_up,
    v_down,
    load_sem,
    send_one,
    recv_one,
    send_two,
    recv_two,
    col_send,
    col_recv,
    share_send,
    share_recv,
    sib_send,
    sib_recv,
    y_send,
    y_recv,
    up_send,
    up_recv,
    down_send,
    down_recv,
):
    me = lax.axis_index("dev")
    depth = n // 4
    z, y, k = me // 4, (me // 2) % 2, me % 2
    t_dev = attended.shape[0]
    half = t_dev // HALVES
    width = out_weight.shape[1]
    ff = w_gate.shape[1]
    model = attended.shape[1]

    def at(zz, yy, kk):
        return zz * 4 + yy * 2 + kk

    sib, beside = at(z, y, 1 - k), at(z, 1 - y, k)

    def remote(src, dst, send, recv, target):
        return pltpu.make_async_remote_copy(
            src_ref=src,
            dst_ref=dst,
            send_sem=send,
            recv_sem=recv,
            device_id={"dev": target},
            device_id_type=MESH,
        )

    loads = [
        pltpu.make_async_copy(out_weight, v_out, load_sem.at[0]),
        pltpu.make_async_copy(w_gate, v_gate, load_sem.at[1]),
        pltpu.make_async_copy(w_up, v_up, load_sem.at[2]),
        pltpu.make_async_copy(w_down, v_down, load_sem.at[3]),
    ]
    for load in loads:
        load.start()
    rows_one[me] = attended[...]

    barrier = pltpu.get_barrier_semaphore()

    def greet(i, _):
        pl.semaphore_signal(
            barrier, inc=1, device_id={"dev": lax.rem(me + i, n)}, device_id_type=MESH
        )
        return 0

    lax.fori_loop(1, n, greet, 0)
    pl.semaphore_wait(barrier, n - 1)

    def order(j):
        near = jnp.minimum(z, depth - 1 - z)
        both = j <= 2 * near
        dist = jnp.where(both, (j + 1) // 2, j - near)
        rising = jnp.where(z < depth - 1 - z, 1, -1)
        sign = jnp.where(both, jnp.where(j % 2 == 1, -1, 1), rising)
        return z + sign * dist

    def gather(buf, send, recv, use):
        def copy(b, h, way, target):
            piece = buf.at[b, pl.ds(h * half, half), :]
            return remote(piece, piece, send.at[b, h, way], recv.at[b, h], target)

        def sends(zj, b, h, act):
            @pl.when((zj <= z) & (z < depth - 1))
            def _():
                act(copy(b, h, UP, at(z + 1, y, k)))

            @pl.when((zj >= z) & (z > 0))
            def _():
                act(copy(b, h, DOWN, at(z - 1, y, k)))

            act(copy(b, h, ACROSS, beside))
            act(copy(b, h, SIBLING, sib))

        def stage(j, _):
            for h in range(HALVES):

                @pl.when(j < depth)
                def _():
                    zj = order(j)
                    b = at(zj, y, k)

                    @pl.when(j > 0)
                    def _():
                        copy(b, h, SIBLING, sib).wait_recv()

                    sends(zj, b, h, lambda c: c.start())

                @pl.when((j >= 1) & (j <= depth))
                def _():
                    b = at(order(j - 1), 1 - y, k)
                    copy(b, h, SIBLING, sib).wait_recv()
                    copy(b, h, SIBLING, sib).start()

                @pl.when(j >= 2)
                def _():
                    zj = order(j - 2)
                    if h == 0:
                        for yy in range(2):
                            for hh in range(HALVES):
                                copy(at(zj, yy, 1 - k), hh, SIBLING, sib).wait_recv()
                    use(zj, h)

            return 0

        lax.fori_loop(0, depth + 2, stage, 0)

        def drain():
            def one(j, _):
                zj = order(j)
                for h in range(HALVES):
                    sends(zj, at(zj, y, k), h, lambda c: c.wait_send())
                    copy(at(zj, 1 - y, k), h, SIBLING, sib).wait_send()
                return 0

            lax.fori_loop(0, depth, one, 0)

        return drain

    def share_copy(b, slot):
        return remote(share.at[b], share_in.at[slot], share_send.at[b], share_recv.at[slot], b)

    def col_copy(b, slot):
        return remote(cols.at[b], arrived.at[slot], col_send.at[b], col_recv.at[slot], b)

    share_in[me] = share[me]

    def give_share(i, _):
        share_copy(lax.rem(me + i, n), me).start()
        return 0

    lax.fori_loop(1, n, give_share, 0)
    loads[0].wait()

    def project(zj, h):
        if h > 0:
            return
        x = rows_one[pl.ds(zj * 4, 4)].reshape(4 * t_dev, model)
        c = jnp.dot(x, v_out[...], preferred_element_type=jnp.float32).astype(jnp.bfloat16)
        cols[pl.ds(zj * 4, 4)] = c.reshape(4, t_dev, width)
        for q in range(4):
            b = zj * 4 + q

            @pl.when(b != me)
            def _():
                col_copy(b, me).start()

    drain_one = gather(rows_one, send_one, recv_one, project)
    arrived[me] = cols[me]

    def take(i, _):
        s = lax.rem(me + i, n)
        col_copy(s, s).wait_recv()
        share_copy(s, s).wait_recv()
        return 0

    lax.fori_loop(1, n, take, 0)
    squares = jnp.zeros((t_dev, width), jnp.float32)
    for s in range(n):
        cut = pl.ds(s * width, width)
        piece = residual[:, cut].astype(jnp.float32) + arrived[s].astype(jnp.float32)
        stream[:, cut] = piece
        squares += piece * piece
    scale = lax.rsqrt(jnp.sum(squares, axis=1, keepdims=True) * (1.0 / model) + 1e-06)
    for s in range(n):
        cut = pl.ds(s * width, width)
        rows_two[me, :, cut] = (
            stream[:, cut] * scale * gain[:, cut].astype(jnp.float32)
        ).astype(jnp.bfloat16)
    for load in loads[1:]:
        load.wait()

    def sib_copy(b):
        return remote(part.at[b], from_sib.at[b // 2], sib_send.at[b // 2], sib_recv.at[b // 2], sib)

    tile, wide = 256, 512
    lanes = share_in.shape[2]
    eye = lax.broadcasted_iota(jnp.int32, (t_dev, lanes), 0) == lax.broadcasted_iota(
        jnp.int32, (t_dev, lanes), 1
    )

    def expert(zj, h):
        def hidden(t, _):
            x = rows_two[pl.ds(zj * 4, 4)].reshape(4 * t_dev, model)
            cut = pl.ds(pl.multiple_of(t * tile, tile), tile)
            g = jnp.dot(x, v_gate[:, cut], preferred_element_type=jnp.float32)
            u = jnp.dot(x, v_up[:, cut], preferred_element_type=jnp.float32)
            inner[:, cut] = (g / (1.0 + jnp.exp(-g)) * u).astype(jnp.bfloat16)
            return 0

        if h == 0:
            lax.fori_loop(0, ff // tile, hidden, 0)
            return
        weights = jnp.concatenate(
            [
                jnp.sum(
                    jnp.where(eye, share_in[zj * 4 + q, 0:1, :], 0.0), axis=1, keepdims=True
                )
                for q in range(4)
            ],
            axis=0,
        )

        def outward(t, _):
            cut = pl.ds(pl.multiple_of(t * wide, wide), wide)
            o = jnp.dot(inner[...], v_down[:, cut], preferred_element_type=jnp.float32)
            part[pl.ds(zj * 4, 4), :, cut] = (
                (o * weights).astype(jnp.bfloat16).reshape(4, t_dev, wide)
            )
            return 0

        lax.fori_loop(0, model // wide, outward, 0)
        for yy in range(2):
            sib_copy(at(zj, yy, 1 - k)).start()

    drain_two = gather(rows_two, send_two, recv_two, expert)

    def cut_rows(h):
        return pl.ds(h * half, half)

    def add(b, h, other):
        rows = cut_rows(h)
        part[b, rows, :] = (
            part[b, rows, :].astype(jnp.float32) + other.astype(jnp.float32)
        ).astype(jnp.bfloat16)

    def line_copy(src, dst, send, recv, zb, h, target):
        rows = cut_rows(h)
        return remote(
            part.at[src, rows, :], dst.at[zb, rows, :], send.at[zb, h], recv.at[zb, h], target
        )

    def y_copy(zb, h):
        return line_copy(at(zb, 1 - y, k), from_y, y_send, y_recv, zb, h, beside)

    def up_copy(zb, h):
        return line_copy(at(zb, y, k), from_below, up_send, up_recv, zb, h, at(z + 1, y, k))

    def down_copy(zb, h):
        return line_copy(at(zb, y, k), from_above, down_send, down_recv, zb, h, at(z - 1, y, k))

    def sides(t, act):
        for h in range(HALVES):

            @pl.when(z + t < depth)
            def _():
                act(z + t, h, True)

            @pl.when(z - t >= 0)
            def _():
                act(z - t, h, False)

    def cross(zb, h):
        away, here = at(zb, 1 - y, k), at(zb, y, k)
        if h == 0:
            sib_copy(away).wait_recv()
        add(away, h, from_sib[zb * 2 + 1 - y, cut_rows(h), :])
        y_copy(zb, h).start()

    def cross_level(i, _):
        sides(depth - 1 - i, lambda zb, h, rising: cross(zb, h))
        return 0

    lax.fori_loop(0, depth - 1, cross_level, 0)
    for h in range(HALVES):
        cross(z, h)

    def home(zb, _):
        here = at(zb, y, k)
        sib_copy(here).wait_recv()
        for h in range(HALVES):
            add(here, h, from_sib[zb * 2 + y, cut_rows(h), :])
        return 0

    lax.fori_loop(0, depth, home, 0)

    def along(zb, h, rising):
        y_copy(zb, h).wait_recv()
        here, rows = at(zb, y, k), cut_rows(h)
        if rising:

            @pl.when(z == 0)
            def _():
                add(here, h, from_y[zb, rows, :])

            @pl.when(z > 0)
            def _():
                up_copy(zb, h).wait_recv()
                add(
                    here,
                    h,
                    from_y[zb, rows, :].astype(jnp.float32)
                    + from_below[zb, rows, :].astype(jnp.float32),
                )

            up_copy(zb, h).start()
        else:

            @pl.when(z == depth - 1)
            def _():
                add(here, h, from_y[zb, rows, :])

            @pl.when(z < depth - 1)
            def _():
                down_copy(zb, h).wait_recv()
                add(
                    here,
                    h,
                    from_y[zb, rows, :].astype(jnp.float32)
                    + from_above[zb, rows, :].astype(jnp.float32),
                )

            down_copy(zb, h).start()

    def along_level(i, _):
        sides(depth - 1 - i, along)
        return 0

    lax.fori_loop(0, depth - 1, along_level, 0)
    for h in range(HALVES):
        y_copy(z, h).wait_recv()
    stream[...] += part[me].astype(jnp.float32) + from_y[z].astype(jnp.float32)

    @pl.when(z > 0)
    def _():
        for h in range(HALVES):
            up_copy(z, h).wait_recv()
        stream[...] += from_below[z].astype(jnp.float32)

    @pl.when(z < depth - 1)
    def _():
        for h in range(HALVES):
            down_copy(z, h).wait_recv()
        stream[...] += from_above[z].astype(jnp.float32)

    out[...] = stream[...].astype(jnp.bfloat16)

    drain_one()
    drain_two()

    def sent(i, _):
        b = lax.rem(me + i, n)
        share_copy(b, me).wait_send()
        col_copy(b, me).wait_send()
        return 0

    lax.fori_loop(1, n, sent, 0)

    def sent_line(zb, _):
        for yy in range(2):
            sib_copy(at(zb, yy, 1 - k)).wait_send()
        for h in range(HALVES):
            y_copy(zb, h).wait_send()

            @pl.when(zb > z)
            def _():
                up_copy(zb, h).wait_send()

            @pl.when(zb < z)
            def _():
                down_copy(zb, h).wait_send()

        return 0

    lax.fori_loop(0, depth, sent_line, 0)


def per_device(
    queries,
    keys,
    values,
    lengths,
    residual,
    out_weight,
    norm_gain,
    expert_ids,
    routed_gate_weight,
    w_gate,
    w_up,
    w_down,
):
    n = lax.axis_size("dev")
    depth = n // 4
    t_dev, model = residual.shape
    width = out_weight.shape[1]
    ff = w_gate.shape[2]
    attended = attend(queries, keys, values, lengths)
    experts = jnp.arange(n, dtype=jnp.int32)
    named = expert_ids[None, :, :] == experts[:, None, None]
    share = jnp.sum(jnp.where(named, routed_gate_weight[None], 0.0), axis=2)
    share = jnp.zeros((n, 8, 128), jnp.float32).at[:, 0, :t_dev].set(share)
    vmem, anywhere = pl.BlockSpec(memory_space=pltpu.VMEM), pl.BlockSpec(memory_space=pl.ANY)
    b16, f32 = jnp.bfloat16, jnp.float32
    dma = pltpu.SemaphoreType.DMA
    return pl.pallas_call(
        functools.partial(layer_kernel, n),
        out_shape=jax.ShapeDtypeStruct((t_dev, model), b16),
        in_specs=[vmem] * 4 + [anywhere] * 4,
        out_specs=vmem,
        scratch_shapes=[
            pltpu.VMEM((n, t_dev, model), b16),
            pltpu.VMEM((n, t_dev, model), b16),
            pltpu.VMEM((n, t_dev, width), b16),
            pltpu.VMEM((n, t_dev, width), b16),
            pltpu.VMEM((n, 8, 128), f32),
            pltpu.VMEM((t_dev, model), f32),
            pltpu.VMEM((4 * t_dev, ff), b16),
            pltpu.VMEM((n, t_dev, model), b16),
            pltpu.VMEM((n // 2, t_dev, model), b16),
            pltpu.VMEM((depth, t_dev, model), b16),
            pltpu.VMEM((depth, t_dev, model), b16),
            pltpu.VMEM((depth, t_dev, model), b16),
            pltpu.VMEM((model, width), b16),
            pltpu.VMEM((model, ff), b16),
            pltpu.VMEM((model, ff), b16),
            pltpu.VMEM((ff, model), b16),
            dma((4,)),
            dma((n, HALVES, 4)),
            dma((n, HALVES)),
            dma((n, HALVES, 4)),
            dma((n, HALVES)),
            dma((n,)),
            dma((n,)),
            dma((n,)),
            dma((n,)),
            dma((n // 2,)),
            dma((n // 2,)),
            dma((depth, HALVES)),
            dma((depth, HALVES)),
            dma((depth, HALVES)),
            dma((depth, HALVES)),
            dma((depth, HALVES)),
            dma((depth, HALVES)),
        ],
        compiler_params=pltpu.CompilerParams(
            collective_id=0, has_side_effects=True, vmem_limit_bytes=62 * 1024 * 1024
        ),
    )(
        attended,
        residual,
        norm_gain.reshape(1, model),
        share,
        out_weight,
        w_gate[0],
        w_up[0],
        w_down[0],
    )


def solution(mesh):
    in_specs = (
        P(("groups", "dev"), None),
        P(("groups", "dev"), None, None),
        P(("groups", "dev"), None, None),
        P(("groups", "dev")),
        P(("groups", "dev"), None),
        P(None, "dev"),
        P(),
        P(("groups", "dev"), None),
        P(("groups", "dev"), None),
        P("dev", None, None),
        P("dev", None, None),
        P("dev", None, None),
    )
    out_specs = P(("groups", "dev"), None)
    return jax.shard_map(
        per_device, mesh=mesh, in_specs=in_specs, out_specs=out_specs, check_vma=False
    )
```

```python
import functools
import math

import jax
import jax.numpy as jnp
from jax import lax
from jax.experimental import pallas as pl
from jax.experimental.pallas import tpu as pltpu
from jax.sharding import PartitionSpec as P

HQ = 32
KVH = 2
HD = 128


MESH = pl.DeviceIdType.MESH
HALVES = 2
TOGETHER = 8
UP, DOWN, ACROSS, SIBLING = 0, 1, 2, 3


def layer_kernel(
    n,
    lengths,
    queries,
    residual,
    gain,
    ids,
    routed,
    keys,
    values,
    out_weight,
    w_gate,
    w_up,
    w_down,
    out,
    heads_in,
    heads_out,
    v_keys,
    v_values,
    share,
    rows_one,
    rows_two,
    cols,
    arrived,
    share_in,
    stream,
    inner,
    part,
    from_sib,
    from_y,
    from_below,
    from_above,
    v_out,
    v_gate,
    v_up,
    v_down,
    load_sem,
    kv_sem,
    send_one,
    recv_one,
    send_two,
    recv_two,
    col_send,
    col_recv,
    share_send,
    share_recv,
    sib_send,
    sib_recv,
    y_send,
    y_recv,
    up_send,
    up_recv,
    down_send,
    down_recv,
):
    me = lax.axis_index("dev")
    depth = n // 4
    z, y, k = me // 4, (me // 2) % 2, me % 2
    t_dev = queries.shape[0]
    half = t_dev // HALVES
    width = out_weight.shape[1]
    ff = w_gate.shape[1]
    model = queries.shape[1]
    positions = keys.shape[1]
    groups = HQ // KVH

    def at(zz, yy, kk):
        return zz * 4 + yy * 2 + kk

    sib, beside = at(z, y, 1 - k), at(z, 1 - y, k)

    def remote(src, dst, send, recv, target):
        return pltpu.make_async_remote_copy(
            src_ref=src,
            dst_ref=dst,
            send_sem=send,
            recv_sem=recv,
            device_id={"dev": target},
            device_id_type=MESH,
        )

    loads = [
        pltpu.make_async_copy(out_weight, v_out, load_sem.at[0]),
        pltpu.make_async_copy(w_gate, v_gate, load_sem.at[1]),
        pltpu.make_async_copy(w_up, v_up, load_sem.at[2]),
        pltpu.make_async_copy(w_down, v_down, load_sem.at[3]),
    ]
    def kv_loads(h):
        rows = pl.ds(h * half, half)
        return (
            pltpu.make_async_copy(keys.at[rows], v_keys.at[rows], kv_sem.at[h, 0]),
            pltpu.make_async_copy(values.at[rows], v_values.at[rows], kv_sem.at[h, 1]),
        )

    for h in range(HALVES):
        for load in kv_loads(h):
            load.start()
    for load in loads:
        load.start()

    barrier = pltpu.get_barrier_semaphore()

    def greet(i, _):
        pl.semaphore_signal(
            barrier, inc=1, device_id={"dev": lax.rem(me + i, n)}, device_id_type=MESH
        )
        return 0

    lax.fori_loop(1, n, greet, 0)

    expert_lane = lax.broadcasted_iota(jnp.int32, (t_dev, 128), 1)
    dense = jnp.zeros((t_dev, 128), jnp.float32)
    for i in range(ids.shape[1]):
        dense += jnp.where(ids[:, i : i + 1] == expert_lane, routed[:, i : i + 1], 0.0)
    turned = jnp.concatenate([dense, jnp.zeros((128 - t_dev, 128), jnp.float32)], axis=0).T
    for e in range(n):
        share[e] = jnp.broadcast_to(turned[e : e + 1, :], (8, 128))

    for i in range(HQ):
        heads_in[:, i, :] = queries[:, i * HD : (i + 1) * HD].astype(jnp.float32)

    def attend_half(h):
        for load in kv_loads(h):
            load.wait()
        low = lax.broadcasted_iota(jnp.int32, (HQ, HD), 0) < groups
        place = lax.broadcasted_iota(jnp.int32, (HQ, positions), 1)

        def some(i, _):
            for u in range(TOGETHER):
                b = h * half + i * TOGETHER + u
                q = heads_in[b]
                q = jnp.concatenate(
                    [jnp.where(low, q, 0.0), jnp.where(low, 0.0, q)], axis=1
                ).astype(jnp.bfloat16)
                score = lax.dot_general(
                    q, v_keys[b], (((1,), (1,)), ((), ())), preferred_element_type=jnp.float32
                ) * (1.0 / math.sqrt(HD))
                score = jnp.where(place < lengths[b], score, jnp.float32(-1e30))
                w = jnp.exp(score - jnp.max(score, axis=1, keepdims=True))
                probs = (w / jnp.sum(w, axis=1, keepdims=True)).astype(jnp.bfloat16)
                o = jnp.dot(probs, v_values[b], preferred_element_type=jnp.float32)
                heads_out[b] = jnp.where(low, o[:, :HD], o[:, HD:])
            return 0

        lax.fori_loop(0, half // TOGETHER, some, 0)
        rows = pl.ds(h * half, half)
        for i in range(HQ):
            rows_one[me, rows, i * HD : (i + 1) * HD] = heads_out[rows, i, :].astype(jnp.bfloat16)

    attend_half(0)
    pl.semaphore_wait(barrier, n - 1)

    def order(j):
        near = jnp.minimum(z, depth - 1 - z)
        both = j <= 2 * near
        dist = jnp.where(both, (j + 1) // 2, j - near)
        rising = jnp.where(z < depth - 1 - z, 1, -1)
        sign = jnp.where(both, jnp.where(j % 2 == 1, -1, 1), rising)
        return z + sign * dist

    def gather(buf, send, recv, use, prepare=None):
        def copy(b, h, way, target):
            piece = buf.at[b, pl.ds(h * half, half), :]
            return remote(piece, piece, send.at[b, h, way], recv.at[b, h], target)

        def sends(zj, b, h, act):
            @pl.when((zj <= z) & (z < depth - 1))
            def _():
                act(copy(b, h, UP, at(z + 1, y, k)))

            @pl.when((zj >= z) & (z > 0))
            def _():
                act(copy(b, h, DOWN, at(z - 1, y, k)))

            act(copy(b, h, ACROSS, beside))
            act(copy(b, h, SIBLING, sib))

        def stage(j, _):
            for h in range(HALVES):

                @pl.when(j < depth)
                def _():
                    zj = order(j)
                    b = at(zj, y, k)

                    @pl.when(j > 0)
                    def _():
                        copy(b, h, SIBLING, sib).wait_recv()

                    if prepare is not None and h > 0:

                        @pl.when(j == 0)
                        def _():
                            prepare(h)

                    sends(zj, b, h, lambda c: c.start())

                @pl.when((j >= 1) & (j <= depth))
                def _():
                    b = at(order(j - 1), 1 - y, k)
                    copy(b, h, SIBLING, sib).wait_recv()
                    copy(b, h, SIBLING, sib).start()

                @pl.when(j >= 2)
                def _():
                    zj = order(j - 2)
                    if h == 0:
                        for yy in range(2):
                            for hh in range(HALVES):
                                copy(at(zj, yy, 1 - k), hh, SIBLING, sib).wait_recv()
                    use(zj, h)

            return 0

        lax.fori_loop(0, depth + 2, stage, 0)

        def drain():
            def one(j, _):
                zj = order(j)
                for h in range(HALVES):
                    sends(zj, at(zj, y, k), h, lambda c: c.wait_send())
                    copy(at(zj, 1 - y, k), h, SIBLING, sib).wait_send()
                return 0

            lax.fori_loop(0, depth, one, 0)

        return drain

    def share_copy(b, slot):
        return remote(share.at[b], share_in.at[slot], share_send.at[b], share_recv.at[slot], b)

    def col_copy(b, slot):
        return remote(cols.at[b], arrived.at[slot], col_send.at[b], col_recv.at[slot], b)

    share_in[me] = share[me]

    def give_share(i, _):
        share_copy(lax.rem(me + i, n), me).start()
        return 0

    lax.fori_loop(1, n, give_share, 0)
    loads[0].wait()

    def project(zj, h):
        if h > 0:
            return
        x = rows_one[pl.ds(zj * 4, 4)].reshape(4 * t_dev, model)
        c = jnp.dot(x, v_out[...], preferred_element_type=jnp.float32).astype(jnp.bfloat16)
        cols[pl.ds(zj * 4, 4)] = c.reshape(4, t_dev, width)
        for q in range(4):
            b = zj * 4 + q

            @pl.when(b != me)
            def _():
                col_copy(b, me).start()

    drain_one = gather(rows_one, send_one, recv_one, project, attend_half)
    arrived[me] = cols[me]

    def take(i, _):
        s = lax.rem(me + i, n)
        col_copy(s, s).wait_recv()
        share_copy(s, s).wait_recv()
        return 0

    lax.fori_loop(1, n, take, 0)
    squares = jnp.zeros((t_dev, width), jnp.float32)
    for s in range(n):
        cut = pl.ds(s * width, width)
        piece = residual[:, cut].astype(jnp.float32) + arrived[s].astype(jnp.float32)
        stream[:, cut] = piece
        squares += piece * piece
    scale = lax.rsqrt(jnp.sum(squares, axis=1, keepdims=True) * (1.0 / model) + 1e-06)
    for s in range(n):
        cut = pl.ds(s * width, width)
        rows_two[me, :, cut] = (
            stream[:, cut] * scale * gain[:, cut].astype(jnp.float32)
        ).astype(jnp.bfloat16)
    for load in loads[1:]:
        load.wait()

    def sib_copy(b):
        return remote(part.at[b], from_sib.at[b // 2], sib_send.at[b // 2], sib_recv.at[b // 2], sib)

    tile, wide = 256, 512
    lanes = share_in.shape[2]
    eye = lax.broadcasted_iota(jnp.int32, (t_dev, lanes), 0) == lax.broadcasted_iota(
        jnp.int32, (t_dev, lanes), 1
    )

    def expert(zj, h):
        def hidden(t, _):
            x = rows_two[pl.ds(zj * 4, 4)].reshape(4 * t_dev, model)
            cut = pl.ds(pl.multiple_of(t * tile, tile), tile)
            g = jnp.dot(x, v_gate[:, cut], preferred_element_type=jnp.float32)
            u = jnp.dot(x, v_up[:, cut], preferred_element_type=jnp.float32)
            inner[:, cut] = (g / (1.0 + jnp.exp(-g)) * u).astype(jnp.bfloat16)
            return 0

        if h == 0:
            lax.fori_loop(0, ff // tile, hidden, 0)
            return
        weights = jnp.concatenate(
            [
                jnp.sum(
                    jnp.where(eye, share_in[zj * 4 + q, 0:1, :], 0.0), axis=1, keepdims=True
                )
                for q in range(4)
            ],
            axis=0,
        )

        def outward(t, _):
            cut = pl.ds(pl.multiple_of(t * wide, wide), wide)
            o = jnp.dot(inner[...], v_down[:, cut], preferred_element_type=jnp.float32)
            part[pl.ds(zj * 4, 4), :, cut] = (
                (o * weights).astype(jnp.bfloat16).reshape(4, t_dev, wide)
            )
            return 0

        lax.fori_loop(0, model // wide, outward, 0)
        for yy in range(2):
            sib_copy(at(zj, yy, 1 - k)).start()

    drain_two = gather(rows_two, send_two, recv_two, expert)

    def cut_rows(h):
        return pl.ds(h * half, half)

    def add(b, h, other):
        rows = cut_rows(h)
        part[b, rows, :] = (
            part[b, rows, :].astype(jnp.float32) + other.astype(jnp.float32)
        ).astype(jnp.bfloat16)

    def line_copy(src, dst, send, recv, zb, h, target):
        rows = cut_rows(h)
        return remote(
            part.at[src, rows, :], dst.at[zb, rows, :], send.at[zb, h], recv.at[zb, h], target
        )

    def y_copy(zb, h):
        return line_copy(at(zb, 1 - y, k), from_y, y_send, y_recv, zb, h, beside)

    def up_copy(zb, h):
        return line_copy(at(zb, y, k), from_below, up_send, up_recv, zb, h, at(z + 1, y, k))

    def down_copy(zb, h):
        return line_copy(at(zb, y, k), from_above, down_send, down_recv, zb, h, at(z - 1, y, k))

    def sides(t, act):
        for h in range(HALVES):

            @pl.when(z + t < depth)
            def _():
                act(z + t, h, True)

            @pl.when(z - t >= 0)
            def _():
                act(z - t, h, False)

    def cross(zb, h):
        away, here = at(zb, 1 - y, k), at(zb, y, k)
        if h == 0:
            sib_copy(away).wait_recv()
        add(away, h, from_sib[zb * 2 + 1 - y, cut_rows(h), :])
        y_copy(zb, h).start()

    def cross_level(i, _):
        sides(depth - 1 - i, lambda zb, h, rising: cross(zb, h))
        return 0

    lax.fori_loop(0, depth - 1, cross_level, 0)
    for h in range(HALVES):
        cross(z, h)

    def home(zb, _):
        here = at(zb, y, k)
        sib_copy(here).wait_recv()
        for h in range(HALVES):
            add(here, h, from_sib[zb * 2 + y, cut_rows(h), :])
        return 0

    lax.fori_loop(0, depth, home, 0)

    def along(zb, h, rising):
        y_copy(zb, h).wait_recv()
        here, rows = at(zb, y, k), cut_rows(h)
        if rising:

            @pl.when(z == 0)
            def _():
                add(here, h, from_y[zb, rows, :])

            @pl.when(z > 0)
            def _():
                up_copy(zb, h).wait_recv()
                add(
                    here,
                    h,
                    from_y[zb, rows, :].astype(jnp.float32)
                    + from_below[zb, rows, :].astype(jnp.float32),
                )

            up_copy(zb, h).start()
        else:

            @pl.when(z == depth - 1)
            def _():
                add(here, h, from_y[zb, rows, :])

            @pl.when(z < depth - 1)
            def _():
                down_copy(zb, h).wait_recv()
                add(
                    here,
                    h,
                    from_y[zb, rows, :].astype(jnp.float32)
                    + from_above[zb, rows, :].astype(jnp.float32),
                )

            down_copy(zb, h).start()

    def along_level(i, _):
        sides(depth - 1 - i, along)
        return 0

    lax.fori_loop(0, depth - 1, along_level, 0)
    for h in range(HALVES):
        y_copy(z, h).wait_recv()
    stream[...] += part[me].astype(jnp.float32) + from_y[z].astype(jnp.float32)

    @pl.when(z > 0)
    def _():
        for h in range(HALVES):
            up_copy(z, h).wait_recv()
        stream[...] += from_below[z].astype(jnp.float32)

    @pl.when(z < depth - 1)
    def _():
        for h in range(HALVES):
            down_copy(z, h).wait_recv()
        stream[...] += from_above[z].astype(jnp.float32)

    out[...] = stream[...].astype(jnp.bfloat16)

    drain_one()
    drain_two()

    def sent(i, _):
        b = lax.rem(me + i, n)
        share_copy(b, me).wait_send()
        col_copy(b, me).wait_send()
        return 0

    lax.fori_loop(1, n, sent, 0)

    def sent_line(zb, _):
        for yy in range(2):
            sib_copy(at(zb, yy, 1 - k)).wait_send()
        for h in range(HALVES):
            y_copy(zb, h).wait_send()

            @pl.when(zb > z)
            def _():
                up_copy(zb, h).wait_send()

            @pl.when(zb < z)
            def _():
                down_copy(zb, h).wait_send()

        return 0

    lax.fori_loop(0, depth, sent_line, 0)


def per_device(
    queries,
    keys,
    values,
    lengths,
    residual,
    out_weight,
    norm_gain,
    expert_ids,
    routed_gate_weight,
    w_gate,
    w_up,
    w_down,
):
    n = lax.axis_size("dev")
    depth = n // 4
    t_dev, model = residual.shape
    width = out_weight.shape[1]
    ff = w_gate.shape[2]
    vmem, anywhere = pl.BlockSpec(memory_space=pltpu.VMEM), pl.BlockSpec(memory_space=pl.ANY)
    b16, f32 = jnp.bfloat16, jnp.float32
    dma = pltpu.SemaphoreType.DMA
    return pl.pallas_call(
        functools.partial(layer_kernel, n),
        out_shape=jax.ShapeDtypeStruct((t_dev, model), b16),
        in_specs=[pl.BlockSpec(memory_space=pltpu.SMEM)] + [vmem] * 5 + [anywhere] * 6,
        out_specs=vmem,
        scratch_shapes=[
            pltpu.VMEM((t_dev, HQ, HD), f32),
            pltpu.VMEM((t_dev, HQ, HD), f32),
            pltpu.VMEM(keys.shape, b16),
            pltpu.VMEM(values.shape, b16),
            pltpu.VMEM((n, 8, 128), f32),
            pltpu.VMEM((n, t_dev, model), b16),
            pltpu.VMEM((n, t_dev, model), b16),
            pltpu.VMEM((n, t_dev, width), b16),
            pltpu.VMEM((n, t_dev, width), b16),
            pltpu.VMEM((n, 8, 128), f32),
            pltpu.VMEM((t_dev, model), f32),
            pltpu.VMEM((4 * t_dev, ff), b16),
            pltpu.VMEM((n, t_dev, model), b16),
            pltpu.VMEM((n // 2, t_dev, model), b16),
            pltpu.VMEM((depth, t_dev, model), b16),
            pltpu.VMEM((depth, t_dev, model), b16),
            pltpu.VMEM((depth, t_dev, model), b16),
            pltpu.VMEM((model, width), b16),
            pltpu.VMEM((model, ff), b16),
            pltpu.VMEM((model, ff), b16),
            pltpu.VMEM((ff, model), b16),
            dma((4,)),
            dma((HALVES, 2)),
            dma((n, HALVES, 4)),
            dma((n, HALVES)),
            dma((n, HALVES, 4)),
            dma((n, HALVES)),
            dma((n,)),
            dma((n,)),
            dma((n,)),
            dma((n,)),
            dma((n // 2,)),
            dma((n // 2,)),
            dma((depth, HALVES)),
            dma((depth, HALVES)),
            dma((depth, HALVES)),
            dma((depth, HALVES)),
            dma((depth, HALVES)),
            dma((depth, HALVES)),
        ],
        compiler_params=pltpu.CompilerParams(
            collective_id=0, has_side_effects=True, vmem_limit_bytes=63 * 1024 * 1024
        ),
    )(
        lengths,
        queries,
        residual,
        norm_gain.reshape(1, model),
        expert_ids,
        routed_gate_weight,
        keys,
        values,
        out_weight,
        w_gate[0],
        w_up[0],
        w_down[0],
    )


def solution(mesh):
    in_specs = (
        P(("groups", "dev"), None),
        P(("groups", "dev"), None, None),
        P(("groups", "dev"), None, None),
        P(("groups", "dev")),
        P(("groups", "dev"), None),
        P(None, "dev"),
        P(),
        P(("groups", "dev"), None),
        P(("groups", "dev"), None),
        P("dev", None, None),
        P("dev", None, None),
        P("dev", None, None),
    )
    out_specs = P(("groups", "dev"), None)
    return jax.shard_map(
        per_device, mesh=mesh, in_specs=in_specs, out_specs=out_specs, check_vma=False
    )
```

```python
import functools
import math

import jax
import jax.numpy as jnp
from jax import lax
from jax.experimental import pallas as pl
from jax.experimental.pallas import tpu as pltpu
from jax.sharding import PartitionSpec as P

HQ = 32
KVH = 2
HD = 128


MESH = pl.DeviceIdType.MESH
HALVES = 2
TOGETHER = 16
UP, DOWN, ACROSS, SIBLING = 0, 1, 2, 3


def layer_kernel(
    n,
    lengths,
    queries,
    residual,
    gain,
    ids,
    routed,
    keys,
    values,
    out_weight,
    w_gate,
    w_up,
    w_down,
    out,
    heads_in,
    heads_out,
    v_keys,
    v_values,
    share,
    rows_one,
    rows_two,
    cols,
    arrived,
    share_in,
    stream,
    inner,
    part,
    from_sib,
    from_y,
    from_below,
    from_above,
    v_out,
    v_gate,
    v_up,
    v_down,
    load_sem,
    kv_sem,
    send_one,
    recv_one,
    send_two,
    recv_two,
    col_send,
    col_recv,
    share_send,
    share_recv,
    sib_send,
    sib_recv,
    y_send,
    y_recv,
    up_send,
    up_recv,
    down_send,
    down_recv,
):
    me = lax.axis_index("dev")
    depth = n // 4
    z, y, k = me // 4, (me // 2) % 2, me % 2
    t_dev = queries.shape[0]
    half = t_dev // HALVES
    width = out_weight.shape[1]
    ff = w_gate.shape[1]
    model = queries.shape[1]
    positions = keys.shape[1]
    groups = HQ // KVH

    def at(zz, yy, kk):
        return zz * 4 + yy * 2 + kk

    sib, beside = at(z, y, 1 - k), at(z, 1 - y, k)

    def remote(src, dst, send, recv, target):
        return pltpu.make_async_remote_copy(
            src_ref=src,
            dst_ref=dst,
            send_sem=send,
            recv_sem=recv,
            device_id={"dev": target},
            device_id_type=MESH,
        )

    loads = [
        pltpu.make_async_copy(out_weight, v_out, load_sem.at[0]),
        pltpu.make_async_copy(w_gate, v_gate, load_sem.at[1]),
        pltpu.make_async_copy(w_up, v_up, load_sem.at[2]),
        pltpu.make_async_copy(w_down, v_down, load_sem.at[3]),
    ]
    def kv_loads(h):
        rows = pl.ds(h * half, half)
        return (
            pltpu.make_async_copy(keys.at[rows], v_keys.at[rows], kv_sem.at[h, 0]),
            pltpu.make_async_copy(values.at[rows], v_values.at[rows], kv_sem.at[h, 1]),
        )

    for h in range(HALVES):
        for load in kv_loads(h):
            load.start()
    for load in loads:
        load.start()

    barrier = pltpu.get_barrier_semaphore()

    def greet(i, _):
        pl.semaphore_signal(
            barrier, inc=1, device_id={"dev": lax.rem(me + i, n)}, device_id_type=MESH
        )
        return 0

    lax.fori_loop(1, n, greet, 0)

    empty = jnp.zeros((8, 128 - t_dev), jnp.float32)
    for e in range(n):
        row = jnp.sum(jnp.where(ids[...] == e, routed[...], 0.0), axis=0, keepdims=True)
        share[e] = jnp.concatenate([jnp.broadcast_to(row, (8, t_dev)), empty], axis=1)

    for i in range(HQ):
        heads_in[:, i, :] = queries[:, i * HD : (i + 1) * HD].astype(jnp.float32)

    def attend_half(h):
        for load in kv_loads(h):
            load.wait()
        low = lax.broadcasted_iota(jnp.int32, (HQ, HD), 0) < groups
        place = lax.broadcasted_iota(jnp.int32, (HQ, positions), 1)

        def some(i, _):
            for u in range(TOGETHER):
                b = h * half + i * TOGETHER + u
                q = heads_in[b]
                q = jnp.concatenate(
                    [jnp.where(low, q, 0.0), jnp.where(low, 0.0, q)], axis=1
                ).astype(jnp.bfloat16)
                score = lax.dot_general(
                    q, v_keys[b], (((1,), (1,)), ((), ())), preferred_element_type=jnp.float32
                ) * (1.0 / math.sqrt(HD))
                score = jnp.where(place < lengths[b], score, jnp.float32(-1e30))
                w = jnp.exp(score - jnp.max(score, axis=1, keepdims=True))
                probs = (w / jnp.sum(w, axis=1, keepdims=True)).astype(jnp.bfloat16)
                o = jnp.dot(probs, v_values[b], preferred_element_type=jnp.float32)
                heads_out[b] = jnp.where(low, o[:, :HD], o[:, HD:])
            return 0

        lax.fori_loop(0, half // TOGETHER, some, 0)
        rows = pl.ds(h * half, half)
        for i in range(HQ):
            rows_one[me, rows, i * HD : (i + 1) * HD] = heads_out[rows, i, :].astype(jnp.bfloat16)

    attend_half(0)
    pl.semaphore_wait(barrier, n - 1)

    def order(j):
        near = jnp.minimum(z, depth - 1 - z)
        both = j <= 2 * near
        dist = jnp.where(both, (j + 1) // 2, j - near)
        rising = jnp.where(z < depth - 1 - z, 1, -1)
        sign = jnp.where(both, jnp.where(j % 2 == 1, -1, 1), rising)
        return z + sign * dist

    def gather(buf, send, recv, use, prepare=None):
        def copy(b, h, way, target):
            piece = buf.at[b, pl.ds(h * half, half), :]
            return remote(piece, piece, send.at[b, h, way], recv.at[b, h], target)

        def sends(zj, b, h, act):
            @pl.when((zj <= z) & (z < depth - 1))
            def _():
                act(copy(b, h, UP, at(z + 1, y, k)))

            @pl.when((zj >= z) & (z > 0))
            def _():
                act(copy(b, h, DOWN, at(z - 1, y, k)))

            act(copy(b, h, ACROSS, beside))
            act(copy(b, h, SIBLING, sib))

        def stage(j, _):
            for h in range(HALVES):

                @pl.when(j < depth)
                def _():
                    zj = order(j)
                    b = at(zj, y, k)

                    @pl.when(j > 0)
                    def _():
                        copy(b, h, SIBLING, sib).wait_recv()

                    if prepare is not None and h > 0:

                        @pl.when(j == 0)
                        def _():
                            prepare(h)

                    sends(zj, b, h, lambda c: c.start())

                @pl.when((j >= 1) & (j <= depth))
                def _():
                    b = at(order(j - 1), 1 - y, k)
                    copy(b, h, SIBLING, sib).wait_recv()
                    copy(b, h, SIBLING, sib).start()

                @pl.when(j >= 2)
                def _():
                    zj = order(j - 2)
                    if h == 0:
                        for yy in range(2):
                            for hh in range(HALVES):
                                copy(at(zj, yy, 1 - k), hh, SIBLING, sib).wait_recv()
                    use(zj, h)

            return 0

        lax.fori_loop(0, depth + 2, stage, 0)

        def drain():
            def one(j, _):
                zj = order(j)
                for h in range(HALVES):
                    sends(zj, at(zj, y, k), h, lambda c: c.wait_send())
                    copy(at(zj, 1 - y, k), h, SIBLING, sib).wait_send()
                return 0

            lax.fori_loop(0, depth, one, 0)

        return drain

    def share_copy(b, slot):
        return remote(share.at[b], share_in.at[slot], share_send.at[b], share_recv.at[slot], b)

    def col_copy(b, slot):
        return remote(cols.at[b], arrived.at[slot], col_send.at[b], col_recv.at[slot], b)

    share_in[me] = share[me]

    def give_share(i, _):
        share_copy(lax.rem(me + i, n), me).start()
        return 0

    lax.fori_loop(1, n, give_share, 0)
    loads[0].wait()

    def project(zj, h):
        if h > 0:
            return
        x = rows_one[pl.ds(zj * 4, 4)].reshape(4 * t_dev, model)
        c = jnp.dot(x, v_out[...], preferred_element_type=jnp.float32).astype(jnp.bfloat16)
        cols[pl.ds(zj * 4, 4)] = c.reshape(4, t_dev, width)
        for q in range(4):
            b = zj * 4 + q

            @pl.when(b != me)
            def _():
                col_copy(b, me).start()

    drain_one = gather(rows_one, send_one, recv_one, project, attend_half)
    arrived[me] = cols[me]

    def take(i, _):
        s = lax.rem(me + i, n)
        col_copy(s, s).wait_recv()
        share_copy(s, s).wait_recv()
        return 0

    lax.fori_loop(1, n, take, 0)
    squares = jnp.zeros((t_dev, width), jnp.float32)
    for s in range(n):
        cut = pl.ds(s * width, width)
        piece = residual[:, cut].astype(jnp.float32) + arrived[s].astype(jnp.float32)
        stream[:, cut] = piece
        squares += piece * piece
    scale = lax.rsqrt(jnp.sum(squares, axis=1, keepdims=True) * (1.0 / model) + 1e-06)
    gains = gain[...].astype(jnp.float32).reshape(1, model)
    for s in range(n):
        cut = pl.ds(s * width, width)
        rows_two[me, :, cut] = (
            stream[:, cut] * scale * gains[:, s * width : (s + 1) * width]
        ).astype(jnp.bfloat16)
    for load in loads[1:]:
        load.wait()

    def sib_copy(b):
        return remote(part.at[b], from_sib.at[b // 2], sib_send.at[b // 2], sib_recv.at[b // 2], sib)

    tile, wide = 256, 512
    lanes = share_in.shape[2]
    eye = lax.broadcasted_iota(jnp.int32, (t_dev, lanes), 0) == lax.broadcasted_iota(
        jnp.int32, (t_dev, lanes), 1
    )

    def expert(zj, h):
        def hidden(t, _):
            x = rows_two[pl.ds(zj * 4, 4)].reshape(4 * t_dev, model)
            cut = pl.ds(pl.multiple_of(t * tile, tile), tile)
            g = jnp.dot(x, v_gate[:, cut], preferred_element_type=jnp.float32)
            u = jnp.dot(x, v_up[:, cut], preferred_element_type=jnp.float32)
            inner[:, cut] = (g / (1.0 + jnp.exp(-g)) * u).astype(jnp.bfloat16)
            return 0

        if h == 0:
            lax.fori_loop(0, ff // tile, hidden, 0)
            return
        weights = jnp.concatenate(
            [
                jnp.sum(
                    jnp.where(eye, share_in[zj * 4 + q, 0:1, :], 0.0), axis=1, keepdims=True
                )
                for q in range(4)
            ],
            axis=0,
        )

        def outward(t, _):
            cut = pl.ds(pl.multiple_of(t * wide, wide), wide)
            o = jnp.dot(inner[...], v_down[:, cut], preferred_element_type=jnp.float32)
            part[pl.ds(zj * 4, 4), :, cut] = (
                (o * weights).astype(jnp.bfloat16).reshape(4, t_dev, wide)
            )
            return 0

        lax.fori_loop(0, model // wide, outward, 0)
        for yy in range(2):
            sib_copy(at(zj, yy, 1 - k)).start()

    drain_two = gather(rows_two, send_two, recv_two, expert)

    def cut_rows(h):
        return pl.ds(h * half, half)

    def add(b, h, other):
        rows = cut_rows(h)
        part[b, rows, :] = (
            part[b, rows, :].astype(jnp.float32) + other.astype(jnp.float32)
        ).astype(jnp.bfloat16)

    def line_copy(src, dst, send, recv, zb, h, target):
        rows = cut_rows(h)
        return remote(
            part.at[src, rows, :], dst.at[zb, rows, :], send.at[zb, h], recv.at[zb, h], target
        )

    def y_copy(zb, h):
        return line_copy(at(zb, 1 - y, k), from_y, y_send, y_recv, zb, h, beside)

    def up_copy(zb, h):
        return line_copy(at(zb, y, k), from_below, up_send, up_recv, zb, h, at(z + 1, y, k))

    def down_copy(zb, h):
        return line_copy(at(zb, y, k), from_above, down_send, down_recv, zb, h, at(z - 1, y, k))

    def sides(t, act):
        for h in range(HALVES):

            @pl.when(z + t < depth)
            def _():
                act(z + t, h, True)

            @pl.when(z - t >= 0)
            def _():
                act(z - t, h, False)

    def cross(zb, h):
        away, here = at(zb, 1 - y, k), at(zb, y, k)
        if h == 0:
            sib_copy(away).wait_recv()
        add(away, h, from_sib[zb * 2 + 1 - y, cut_rows(h), :])
        y_copy(zb, h).start()

    def cross_level(i, _):
        sides(depth - 1 - i, lambda zb, h, rising: cross(zb, h))
        return 0

    lax.fori_loop(0, depth - 1, cross_level, 0)
    for h in range(HALVES):
        cross(z, h)

    def home(zb, _):
        here = at(zb, y, k)
        sib_copy(here).wait_recv()
        for h in range(HALVES):
            add(here, h, from_sib[zb * 2 + y, cut_rows(h), :])
        return 0

    lax.fori_loop(0, depth, home, 0)

    def along(zb, h, rising):
        y_copy(zb, h).wait_recv()
        here, rows = at(zb, y, k), cut_rows(h)
        if rising:

            @pl.when(z == 0)
            def _():
                add(here, h, from_y[zb, rows, :])

            @pl.when(z > 0)
            def _():
                up_copy(zb, h).wait_recv()
                add(
                    here,
                    h,
                    from_y[zb, rows, :].astype(jnp.float32)
                    + from_below[zb, rows, :].astype(jnp.float32),
                )

            up_copy(zb, h).start()
        else:

            @pl.when(z == depth - 1)
            def _():
                add(here, h, from_y[zb, rows, :])

            @pl.when(z < depth - 1)
            def _():
                down_copy(zb, h).wait_recv()
                add(
                    here,
                    h,
                    from_y[zb, rows, :].astype(jnp.float32)
                    + from_above[zb, rows, :].astype(jnp.float32),
                )

            down_copy(zb, h).start()

    def along_level(i, _):
        sides(depth - 1 - i, along)
        return 0

    lax.fori_loop(0, depth - 1, along_level, 0)
    for h in range(HALVES):
        y_copy(z, h).wait_recv()
    stream[...] += part[me].astype(jnp.float32) + from_y[z].astype(jnp.float32)

    @pl.when(z > 0)
    def _():
        for h in range(HALVES):
            up_copy(z, h).wait_recv()
        stream[...] += from_below[z].astype(jnp.float32)

    @pl.when(z < depth - 1)
    def _():
        for h in range(HALVES):
            down_copy(z, h).wait_recv()
        stream[...] += from_above[z].astype(jnp.float32)

    out[...] = stream[...].astype(jnp.bfloat16)

    drain_one()
    drain_two()

    def sent(i, _):
        b = lax.rem(me + i, n)
        share_copy(b, me).wait_send()
        col_copy(b, me).wait_send()
        return 0

    lax.fori_loop(1, n, sent, 0)

    def sent_line(zb, _):
        for yy in range(2):
            sib_copy(at(zb, yy, 1 - k)).wait_send()
        for h in range(HALVES):
            y_copy(zb, h).wait_send()

            @pl.when(zb > z)
            def _():
                up_copy(zb, h).wait_send()

            @pl.when(zb < z)
            def _():
                down_copy(zb, h).wait_send()

        return 0

    lax.fori_loop(0, depth, sent_line, 0)


def per_device(
    queries,
    keys,
    values,
    lengths,
    residual,
    out_weight,
    norm_gain,
    expert_ids,
    routed_gate_weight,
    w_gate,
    w_up,
    w_down,
):
    n = lax.axis_size("dev")
    depth = n // 4
    t_dev, model = residual.shape
    width = out_weight.shape[1]
    ff = w_gate.shape[2]
    vmem, anywhere = pl.BlockSpec(memory_space=pltpu.VMEM), pl.BlockSpec(memory_space=pl.ANY)
    b16, f32 = jnp.bfloat16, jnp.float32
    dma = pltpu.SemaphoreType.DMA
    return pl.pallas_call(
        functools.partial(layer_kernel, n),
        out_shape=jax.ShapeDtypeStruct((t_dev, model), b16),
        in_specs=[pl.BlockSpec(memory_space=pltpu.SMEM)] + [vmem] * 5 + [anywhere] * 6,
        out_specs=vmem,
        scratch_shapes=[
            pltpu.VMEM((t_dev, HQ, HD), f32),
            pltpu.VMEM((t_dev, HQ, HD), f32),
            pltpu.VMEM(keys.shape, b16),
            pltpu.VMEM(values.shape, b16),
            pltpu.VMEM((n, 8, 128), f32),
            pltpu.VMEM((n, t_dev, model), b16),
            pltpu.VMEM((n, t_dev, model), b16),
            pltpu.VMEM((n, t_dev, width), b16),
            pltpu.VMEM((n, t_dev, width), b16),
            pltpu.VMEM((n, 8, 128), f32),
            pltpu.VMEM((t_dev, model), f32),
            pltpu.VMEM((4 * t_dev, ff), b16),
            pltpu.VMEM((n, t_dev, model), b16),
            pltpu.VMEM((n // 2, t_dev, model), b16),
            pltpu.VMEM((depth, t_dev, model), b16),
            pltpu.VMEM((depth, t_dev, model), b16),
            pltpu.VMEM((depth, t_dev, model), b16),
            pltpu.VMEM((model, width), b16),
            pltpu.VMEM((model, ff), b16),
            pltpu.VMEM((model, ff), b16),
            pltpu.VMEM((ff, model), b16),
            dma((4,)),
            dma((HALVES, 2)),
            dma((n, HALVES, 4)),
            dma((n, HALVES)),
            dma((n, HALVES, 4)),
            dma((n, HALVES)),
            dma((n,)),
            dma((n,)),
            dma((n,)),
            dma((n,)),
            dma((n // 2,)),
            dma((n // 2,)),
            dma((depth, HALVES)),
            dma((depth, HALVES)),
            dma((depth, HALVES)),
            dma((depth, HALVES)),
            dma((depth, HALVES)),
            dma((depth, HALVES)),
        ],
        compiler_params=pltpu.CompilerParams(
            collective_id=0, has_side_effects=True, vmem_limit_bytes=63 * 1024 * 1024
        ),
    )(
        lengths,
        queries,
        residual,
        norm_gain,
        expert_ids.T,
        routed_gate_weight.T,
        keys,
        values,
        out_weight,
        w_gate[0],
        w_up[0],
        w_down[0],
    )


def solution(mesh):
    in_specs = (
        P(("groups", "dev"), None),
        P(("groups", "dev"), None, None),
        P(("groups", "dev"), None, None),
        P(("groups", "dev")),
        P(("groups", "dev"), None),
        P(None, "dev"),
        P(),
        P(("groups", "dev"), None),
        P(("groups", "dev"), None),
        P("dev", None, None),
        P("dev", None, None),
        P("dev", None, None),
    )
    out_specs = P(("groups", "dev"), None)
    return jax.shard_map(
        per_device, mesh=mesh, in_specs=in_specs, out_specs=out_specs, check_vma=False
    )
```
